256 devices in a mesh: dp: 64 (over z, y, core), tensor: 4 (over x).
Axes of the slice: x: 4, y: 4, z: 8, core: 2. Of those that a mesh axis runs over, the one named last changes fastest.
Arguments:
- queries: bfloat16 [32768, 8192], P(('dp', 'tensor')), may hold values from -20 to 20
- resp_keys: bfloat16 [32768, 1024], P(('dp', 'tensor')), may hold values from -6 to 6
- resp_values: bfloat16 [32768, 1024], P(('dp', 'tensor')), may hold values from -6 to 6
- grad_output: bfloat16 [32768, 8192], P(('dp', 'tensor')), may hold values from -6 to 6
- prompt_keys: bfloat16 [512, 1024], P('dp', 'tensor'), may hold values from -6 to 6
- prompt_values: bfloat16 [512, 1024], P('dp', 'tensor'), may hold values from -6 to 6
- segment_ids: int32 [64, 512], P('dp'), may hold values from 0 to 1, never falling along the last dimension, each value on 1 to 384 neighbouring positions
- response_group: int32 [64, 2], P('dp'), may hold values from 0 to 3
Outputs:
- grad_queries: bfloat16 [32768, 8192], P(('dp', 'tensor'))
- grad_resp_keys: bfloat16 [32768, 1024], P(('dp', 'tensor'))
- grad_resp_values: bfloat16 [32768, 1024], P(('dp', 'tensor'))
- grad_prompt_keys: float32 [512, 1024], P('dp', 'tensor')
- grad_prompt_values: float32 [512, 1024], P('dp', 'tensor')
The draws below stay inside these ranges and needn't reach their ends.
Inputs may be any that keep to these rules, and one draw needn't show every extreme that they name: `segment_ids`: each row holds the 2 responses of one dp index in order, each of 128 to 384 neighbouring positions, their lengths summing to 512.
All inputs are finite; a program needn't handle non-finite values.
Results may differ from the reference program's by a relative error of at most 0.015.
Values may be sent and summed in bfloat16 or wider, within the bound.
No kernel may reach another device: no remote copies, remote signals or barrier semaphores. Data moves between devices by JAX's collectives and lax.ppermute only.
A program may use at most 128 MiB of HBM per device.

```python
import math
import jax
import jax.numpy as jnp
import numpy as np
from jax import lax

HEADS = 64
KV_HEADS = 8
HD = 128
GROUPS = 4
PLEN = 128
TOK_DEV = 512
RESP_DEV = 2
TOKENS = 32768
PTOK = 512
N_DP = 64


def draw_queries(key, part):
    key = jax.random.fold_in(key, 11)
    drawn = jax.random.truncated_normal(key, -6.0, 6.0, (TOKENS, HEADS * HD), jnp.float32)
    return drawn.astype(jnp.bfloat16)


def draw_prompt_keys(key, part):
    key = jax.random.fold_in(key, 23)
    drawn = jax.random.truncated_normal(key, -6.0, 6.0, (GROUPS * PLEN, KV_HEADS * HD), jnp.float32)
    return drawn.astype(jnp.bfloat16)


def with_ends(result, stream_key, least, high):
    dims = result.shape
    index_at = [jax.random.randint(jax.random.fold_in(stream_key, axis), (), 0, dims[axis]) for axis in range(len(dims))]
    result = result.at[tuple(index_at)].set(least)
    longest = dims.index(max(dims))
    index_at[longest] = (index_at[longest] + 1) % dims[longest]
    return result.at[tuple(index_at)].set(high)


def steps_of(key, dims, shards, least, largest):
    def one(position, parts):
        draws = jax.random.uniform(jax.random.fold_in(jax.random.fold_in(key, 6), position), (parts,), jnp.float32, least / len(shards), largest / len(shards))
        return jnp.repeat(jnp.exp(draws), dims[position] // parts).reshape((-1,) + (1,) * (len(dims) - position - 1))

    level = one(*shards[0])
    for cut in shards[1:]:
        level = level * one(*cut)
    return level


def profile(number_of, total, limit, skew):
    weights = [(1 << 20) // math.isqrt(rank ** skew) + 1 for rank in range(2, number_of + 1)]
    surplus, given = total - limit - (number_of - 1), [1] * (number_of - 1)
    while surplus > 0:
        movable = [i for i in range(number_of - 1) if given[i] < limit]
        pool, remaining = sum([weights[i] for i in movable]), surplus
        for i in movable:
            extra = min(limit - given[i], max(1, remaining * weights[i] // pool), surplus)
            given[i] = given[i] + extra
            surplus = surplus - extra
    return np.array([limit] + given)


def uneven(own_key, count, total, most, lean):
    if count == 2:
        one = jax.random.randint(own_key, (), max(1, total - most), min(most, total - 1) + 1)
        return jnp.stack([one, total - one])
    tallies = jnp.asarray(profile(count, total, most, lean), jnp.int32)
    couples = (count - 1) // 2
    source_of, sink = tallies[1:1 + 2 * couples:2], tallies[2:2 + 2 * couples:2]
    margin = jnp.minimum(source_of - 1, most - sink)
    passed = jax.random.randint(jax.random.fold_in(own_key, 1), (couples,), 0, 1 << 20) % (margin + 1)
    tallies = tallies.at[1:1 + 2 * couples:2].set(source_of - passed).at[2:2 + 2 * couples:2].set(sink + passed)
    return tallies[jax.random.permutation(jax.random.fold_in(own_key, 2), count)]


def centred(rng, dims, width, limit, shards=(), held_as=jnp.bfloat16):
    values = jax.random.normal(rng, dims, jnp.float32) * width
    if len(shards) > 0:
        values = steps_of(rng, dims, shards, -0.22, 0.18) * values
    return jnp.clip(values, min=-limit, max=limit).astype(held_as)


def setup_inputs(seed: int = 0) -> dict:
    key_of = jax.random.split(jax.random.key(seed), 9)
    queries = draw_queries(jax.random.fold_in(key_of[8], 71), 0)
    resp_keys = centred(key_of[1], (TOKENS, KV_HEADS * HD), 1.0, 6.0, ((0, 256),))
    resp_values = centred(key_of[2], (TOKENS, KV_HEADS * HD), 1.0, 6.0, ((0, 256),))
    grad_output = centred(key_of[3], (TOKENS, HEADS * HD), 1.0, 6.0, ((0, 256),))
    prompt_keys = draw_prompt_keys(jax.random.fold_in(key_of[8], 71), 0)
    prompt_values = centred(key_of[5], (PTOK, KV_HEADS * HD), 1.0, 6.0, ((0, 64), (1, 4)))
    segment_ids = jax.vmap(lambda own: jnp.searchsorted(jnp.cumsum(uneven(own, RESP_DEV, TOK_DEV, TOK_DEV * 3 // 4, 0)), jnp.arange(TOK_DEV), side="right"))(jax.random.split(key_of[6], N_DP)).reshape((N_DP, TOK_DEV)).astype(jnp.int32)
    response_group = with_ends(jax.random.randint(key_of[7], (N_DP, RESP_DEV), 0, GROUPS), jax.random.fold_in(key_of[7], 1), 0, GROUPS - 1).astype(jnp.int32)
    return dict(queries=queries, resp_keys=resp_keys, resp_values=resp_values, grad_output=grad_output, prompt_keys=prompt_keys, prompt_values=prompt_values, segment_ids=segment_ids, response_group=response_group)


neg_large = -1e30


def head_terms(query_block, grad_block, all_keys, all_values, allowed):
    factor = all_keys.shape[-1] ** -0.5
    key_float = all_keys.astype(jnp.float32)
    value_float = all_values.astype(jnp.float32)
    query_float = query_block.astype(jnp.float32)
    grad_float = grad_block.astype(jnp.float32)
    scores = jnp.einsum("tre,ke->trk", query_float, key_float) * factor
    scores = jnp.where(allowed[:, None, :], scores, neg_large)
    row_max = jnp.max(scores, axis=2, keepdims=True)
    log_total = row_max + jnp.log(jnp.sum(jnp.exp(scores - row_max), axis=2, keepdims=True))
    weights = jnp.exp(scores - log_total)
    probs = weights.astype(jnp.bfloat16)
    prob_float = probs.astype(jnp.float32)
    attended = jnp.einsum("trk,ke->tre", prob_float, value_float)
    deltas = jnp.sum(grad_float * attended, axis=2, keepdims=True)
    grad_probs = jnp.einsum("tre,ke->trk", grad_float, value_float)
    grad_scores = (weights * (grad_probs - deltas)).astype(jnp.bfloat16).astype(jnp.float32)
    grad_query = jnp.einsum("trk,ke->tre", grad_scores, key_float) * factor
    grad_keys = jnp.einsum("trk,tre->ke", grad_scores, query_float) * factor
    grad_values = jnp.einsum("trk,tre->ke", prob_float, grad_float)
    return grad_query, grad_keys, grad_values


def reference(queries, resp_keys, resp_values, grad_output, prompt_keys, prompt_values, segment_ids, response_group):
    per_group = HEADS // KV_HEADS
    group_cols = per_group * HD
    prompt_total = GROUPS * PLEN
    block_queries = queries.reshape(N_DP, TOK_DEV, HEADS * HD)
    block_grads = grad_output.reshape(N_DP, TOK_DEV, HEADS * HD)
    block_keys = resp_keys.reshape(N_DP, TOK_DEV, KV_HEADS * HD)
    block_values = resp_values.reshape(N_DP, TOK_DEV, KV_HEADS * HD)
    prompt_group = jnp.arange(prompt_total, dtype=jnp.int32) // PLEN
    positions = jnp.arange(TOK_DEV, dtype=jnp.int32)

    def one_block(carry, inputs):
        sum_keys, sum_values = carry
        query_here, grad_here, keys_here, values_here, segment_here, group_here = inputs
        token_group = group_here[segment_here]
        prompt_ok = prompt_group[None, :] == token_group[:, None]
        self_ok = (segment_here[:, None] == segment_here[None, :]) & (positions[None, :] <= positions[:, None])
        allowed = jnp.concatenate([prompt_ok, self_ok], axis=1)
        query_parts, key_parts, value_parts, prompt_key_parts, prompt_value_parts = [], [], [], [], []
        for kv_head in range(KV_HEADS):
            query_block = query_here[:, kv_head * group_cols:(kv_head + 1) * group_cols].reshape(TOK_DEV, per_group, HD)
            grad_block = grad_here[:, kv_head * group_cols:(kv_head + 1) * group_cols].reshape(TOK_DEV, per_group, HD)
            all_keys = jnp.concatenate([prompt_keys[:, kv_head * HD:(kv_head + 1) * HD], keys_here[:, kv_head * HD:(kv_head + 1) * HD]], axis=0)
            all_values = jnp.concatenate([prompt_values[:, kv_head * HD:(kv_head + 1) * HD], values_here[:, kv_head * HD:(kv_head + 1) * HD]], axis=0)
            grad_query, grad_keys, grad_values = head_terms(query_block, grad_block, all_keys, all_values, allowed)
            query_parts.append(grad_query.reshape(TOK_DEV, group_cols))
            key_parts.append(grad_keys[prompt_total:])
            value_parts.append(grad_values[prompt_total:])
            prompt_key_parts.append(grad_keys[:prompt_total])
            prompt_value_parts.append(grad_values[:prompt_total])
        out_query = jnp.concatenate(query_parts, axis=1).astype(jnp.bfloat16)
        out_keys = jnp.concatenate(key_parts, axis=1).astype(jnp.bfloat16)
        out_values = jnp.concatenate(value_parts, axis=1).astype(jnp.bfloat16)
        sum_keys = sum_keys + jnp.concatenate(prompt_key_parts, axis=1)
        sum_values = sum_values + jnp.concatenate(prompt_value_parts, axis=1)
        return (sum_keys, sum_values), (out_query, out_keys, out_values)

    start_sums = (jnp.zeros((prompt_total, KV_HEADS * HD), jnp.float32), jnp.zeros((prompt_total, KV_HEADS * HD), jnp.float32))
    (sum_keys, sum_values), (out_query, out_keys, out_values) = lax.scan(
        one_block, start_sums, (block_queries, block_grads, block_keys, block_values, segment_ids, response_group))
    return (out_query.reshape(TOKENS, HEADS * HD), out_keys.reshape(TOKENS, KV_HEADS * HD),
            out_values.reshape(TOKENS, KV_HEADS * HD), sum_keys, sum_values)
```

```python
import functools
import math

import jax
import jax.numpy as jnp
from jax import lax
from jax.experimental import pallas as pl
from jax.experimental.pallas import tpu as pltpu
from jax.sharding import Mesh, PartitionSpec as P

HD = 128
BLK = 128
HEAD_COLS = 1024
KV_HEADS = 8
N_X = 4
FACTOR = HD**-0.5
LOG2_SCALE = FACTOR * math.log2(math.e)
NEG = -1e30
bf16, f32 = jnp.bfloat16, jnp.float32


def dot_nt(a, b):
    return lax.dot_general(a, b, (((1,), (1,)), ((), ())), preferred_element_type=f32)


def dot_nn(a, b):
    return lax.dot_general(a, b, (((1,), (0,)), ((), ())), preferred_element_type=f32)


def attention_kernel(
    sc_ref, q_ref, do_ref, ko_ref, vo_ref, near_ref, far_ref, pr_ref, *refs
):
    dq_ref, own_ref, dnear_ref, dfar_ref, dpr_ref = refs[-5:]
    place, border = sc_ref[1], sc_ref[2]

    def wide(x):
        return jnp.concatenate([x, x], axis=1)

    u = lax.broadcasted_iota(jnp.int32, (3 * BLK, BLK), 0) + (place - 2) * BLK
    t = lax.broadcasted_iota(jnp.int32, (3 * BLK, BLK), 1) + place * BLK
    ok = (u >= 0) & (u <= t) & ((u >= border) == (t >= border))
    bias = wide(jnp.where(ok, 0.0, NEG).astype(f32))
    row_t = lax.broadcasted_iota(jnp.int32, (2 * BLK, HD), 0) % BLK + place * BLK
    first = jnp.where(row_t < border, 1.0, 0.0).astype(bf16)
    second = jnp.where(row_t < border, 0.0, 1.0).astype(bf16)
    lane_t = lax.broadcasted_iota(jnp.int32, (HD, 2 * BLK), 1) % BLK + place * BLK
    lane_first = lane_t < border

    k_r = jnp.concatenate([far_ref[0], near_ref[0], ko_ref[...]], axis=0)
    v_r = jnp.concatenate([far_ref[1], near_ref[1], vo_ref[...]], axis=0)
    k_p = jnp.concatenate([pr_ref[0, 0], pr_ref[1, 0]], axis=1)
    v_p = jnp.concatenate([pr_ref[0, 1], pr_ref[1, 1]], axis=1)
    k_r_t = k_r.T
    k_p_t = k_p.T

    dk_r = dv_r = dk_p = dv_p = None
    for pair in range(4):
        cols = [slice((2 * pair + j) * HD, (2 * pair + j + 1) * HD) for j in range(2)]
        q = jnp.concatenate([q_ref[:, c] for c in cols], axis=0)
        do = jnp.concatenate([do_ref[:, c] for c in cols], axis=0)
        q_two = jnp.concatenate([q * first, q * second], axis=1)
        do_two = jnp.concatenate([do * first, do * second], axis=1)
        s_p = dot_nt(k_p, q_two)
        s_r = dot_nt(k_r, q) + bias
        top = jnp.maximum(
            jnp.max(s_p, axis=0, keepdims=True), jnp.max(s_r, axis=0, keepdims=True)
        )
        e_p = jnp.exp2((s_p - top) * LOG2_SCALE)
        e_r = jnp.exp2((s_r - top) * LOG2_SCALE)
        total = jnp.sum(e_p, axis=0, keepdims=True) + jnp.sum(e_r, axis=0, keepdims=True)
        inv = 1.0 / total
        w_p = e_p * inv
        w_r = e_r * inv
        p_p = w_p.astype(bf16)
        p_r = w_r.astype(bf16)
        g_p = dot_nt(v_p, do_two)
        g_r = dot_nt(v_r, do)
        delta = jnp.sum(p_p.astype(f32) * g_p, axis=0, keepdims=True) + jnp.sum(
            p_r.astype(f32) * g_r, axis=0, keepdims=True
        )
        ds_p = (w_p * (g_p - delta)).astype(bf16)
        ds_r = (w_r * (g_r - delta)).astype(bf16)
        dq_two = dot_nn(k_p_t, ds_p)
        dq_t = dot_nn(k_r_t, ds_r) + jnp.where(lane_first, dq_two[:HD], dq_two[HD:])
        dq = (dq_t * FACTOR).T.astype(bf16)
        for j in range(2):
            dq_ref[:, cols[j]] = dq[j * BLK : (j + 1) * BLK]
        parts = (dot_nn(ds_r, q), dot_nn(p_r, do), dot_nn(ds_p, q_two), dot_nn(p_p, do_two))
        if pair == 0:
            dk_r, dv_r, dk_p, dv_p = parts
        else:
            dk_r, dv_r, dk_p, dv_p = (
                dk_r + parts[0],
                dv_r + parts[1],
                dk_p + parts[2],
                dv_p + parts[3],
            )
    dk_r = dk_r * FACTOR
    dk_p = dk_p * FACTOR
    for j, grad in enumerate((dk_r, dv_r)):
        dfar_ref[j] = grad[:BLK].astype(bf16)
        dnear_ref[j] = grad[BLK : 2 * BLK].astype(bf16)
        own_ref[j] = grad[2 * BLK :]
    for j, grad in enumerate((dk_p, dv_p)):
        dpr_ref[0, j] = grad[:, :HD].astype(bf16)
        dpr_ref[1, j] = grad[:, HD:].astype(bf16)


def attend(scalars, q, do, rk, rv, near, far, prompts, carried):
    def at_head(i, sc):
        return (0, sc[0] + i)

    def pair_at_head(i, sc):
        return (0, 0, sc[0] + i)

    wide_spec = pl.BlockSpec((BLK, HEAD_COLS), at_head)
    one_spec = pl.BlockSpec((BLK, HD), at_head)
    pair_spec = pl.BlockSpec((2, BLK, HD), pair_at_head)
    prompt_spec = pl.BlockSpec((2, 2, BLK, HD), lambda i, sc: (0, 0, 0, i))
    out_shape = (
        jax.ShapeDtypeStruct((BLK, KV_HEADS * HEAD_COLS), bf16),
        jax.ShapeDtypeStruct((2, BLK, KV_HEADS * HD), f32),
        jax.ShapeDtypeStruct((2, BLK, KV_HEADS * HD), bf16),
        jax.ShapeDtypeStruct((2, BLK, KV_HEADS * HD), bf16),
        jax.ShapeDtypeStruct((2, 2, BLK, 2 * HD), bf16),
    )
    in_specs = [
        wide_spec,
        wide_spec,
        one_spec,
        one_spec,
        pair_spec,
        pair_spec,
        prompt_spec,
    ]
    aliases = {}
    operands = [q, do, rk, rv, near, far, prompts]
    if carried is not None:
        for k, array in enumerate(carried):
            aliases[1 + len(operands)] = k
            operands.append(array)
            in_specs.append(pl.BlockSpec(memory_space=pl.ANY))
    return pl.pallas_call(
        attention_kernel,
        out_shape=out_shape,
        grid_spec=pltpu.PrefetchScalarGridSpec(
            num_scalar_prefetch=1,
            grid=(2,),
            in_specs=in_specs,
            out_specs=(wide_spec, pair_spec, pair_spec, pair_spec, prompt_spec),
        ),
        input_output_aliases=aliases,
        compiler_params=pltpu.CompilerParams(vmem_limit_bytes=32 * 1024 * 1024),
        cost_estimate=pl.CostEstimate(
            flops=5 * 2 * 1024 * 512 * 128 * 2 * 2, bytes_accessed=4 << 20, transcendentals=1 << 20
        ),
    )(scalars, *operands)


def shift(a, axis, size, by):
    return lax.ppermute(a, axis, [(i, (i + by) % size) for i in range(size)])


def on_device(q, rk, rv, do, pk, pv, segment_ids, response_group):
    x = lax.axis_index("x")
    core = lax.axis_index("core")
    groups = response_group[0]
    border = jnp.sum((segment_ids[0] == 0).astype(jnp.int32))

    kv = jnp.stack([rk, rv])
    near = lax.ppermute(kv, "x", [(0, 1), (1, 2), (2, 3)])
    far = lax.ppermute(kv, "x", [(0, 2), (1, 3)])

    mine = jnp.stack([pk, pv])
    rows = lax.all_to_all(jnp.broadcast_to(mine, (32, 2, 8, 256)), ("z", "y"), 0, 0)
    other = lax.ppermute(rows, "core", [(0, 1), (1, 0)])
    picked = []
    for r in range(2):
        a = lax.dynamic_slice_in_dim(rows, groups[r] * 8, 8, 0)
        b = lax.dynamic_slice_in_dim(other, groups[r] * 8, 8, 0)
        even = jnp.where(core == 0, a, b)
        odd = jnp.where(core == 0, b, a)
        both = jnp.stack([even, odd], axis=1)
        picked.append(both.transpose(2, 0, 1, 3, 4).reshape(2, BLK, 256))
    own_prompts = jnp.stack(picked)
    slots = [own_prompts] + [shift(own_prompts, "x", N_X, d) for d in range(1, N_X)]

    carried = None
    sent_back = []
    for d in (0, 1, 3, 2):
        head = 2 * ((x - d) % N_X)
        scalars = jnp.stack([head, x, border]).astype(jnp.int32)
        *carried, grad_prompts = attend(scalars, q, do, rk, rv, near, far, slots[d], carried)
        sent_back.append(grad_prompts if d == 0 else shift(grad_prompts, "x", N_X, -d))
    out_q, own, grad_near, grad_far = carried
    back_near = lax.ppermute(grad_near, "x", [(1, 0), (2, 1), (3, 2)])
    back_far = lax.ppermute(grad_far, "x", [(2, 0), (3, 1)])

    summed = sum(part.astype(f32) for part in sent_back)
    dense = jnp.stack(
        [sum(jnp.where(groups[r] == g, summed[r], 0.0) for r in range(2)) for g in range(4)]
    )
    dense = dense.reshape(4, 2, 8, 2, 8, 256).transpose(3, 0, 2, 1, 4, 5)
    dense = dense.reshape(2, 32, 2, 8, 256).astype(bf16)
    keep = lax.dynamic_index_in_dim(dense, core, 0, keepdims=False)
    give = lax.dynamic_index_in_dim(dense, 1 - core, 0, keepdims=False)
    got = lax.ppermute(give, "core", [(0, 1), (1, 0)])
    half = (keep.astype(f32) + got.astype(f32)).astype(bf16)
    spread = lax.all_to_all(half, ("z", "y"), 0, 0)
    out_p = jnp.sum(spread.astype(f32), axis=0)

    out_kv = (own + (back_near.astype(f32) + back_far.astype(f32))).astype(bf16)
    return out_q, out_kv[0], out_kv[1], out_p[0], out_p[1]


def solution(mesh):
    fine = Mesh(mesh.devices.reshape(8, 4, 2, 4), ("z", "y", "core", "x"))
    dp = ("z", "y", "core")
    tokens = P(dp + ("x",), None)
    heads = P(dp, "x")
    per_dp = P(dp, None)
    return jax.shard_map(
        on_device,
        mesh=fine,
        in_specs=(tokens, tokens, tokens, tokens, heads, heads, per_dp, per_dp),
        out_specs=(tokens, tokens, tokens, heads, heads),
        check_vma=False,
    )
```

```python
import functools
import functools
import math

import jax
import jax.numpy as jnp
from jax import lax
from jax.experimental import pallas as pl
from jax.experimental.pallas import tpu as pltpu
from jax.sharding import Mesh, PartitionSpec as P

HD = 128
BLK = 128
HEAD_COLS = 1024
KV_HEADS = 8
N_X = 4
FACTOR = HD**-0.5
LOG2_SCALE = FACTOR * math.log2(math.e)
NEG = -1e30
HEADS_STEP = 2
LANES = HEADS_STEP * BLK
STEPS = 4
bf16, f32 = jnp.bfloat16, jnp.float32


def dot_nt(a, b):
    return lax.dot_general(a, b, (((1,), (1,)), ((), ())), preferred_element_type=f32)


def dot_nn(a, b):
    return lax.dot_general(a, b, (((1,), (0,)), ((), ())), preferred_element_type=f32)


def fold(x, op):
    parts=[x[8*i:8*i+8] for i in range(x.shape[0]//8)]
    while len(parts)>1:
        parts=[op(parts[i],parts[i+1]) if i+1<len(parts) else parts[i] for i in range(0,len(parts),2)]
    return parts[0]
def attention_kernel(
    slot, sc_ref, seg_ref, q_ref, do_ref, kv_ref, near_ref, far_ref, pr_ref, *refs):
    dq_ref, own_ref, dnear_ref, dfar_ref, dpr_ref = refs[-18:-13]
    bias, e0,e1,g0,g1,p0,p1,d0,d1,dkacc,dvacc,dkpacc,dvpacc = refs[-13:]
    ebuf,gbuf,pbuf,dsbuf=(e0,e1),(g0,g1),(p0,p1),(d0,d1)
    place = sc_ref[0]
    border = jnp.sum((seg_ref[...] == 0).astype(jnp.int32), axis=1, keepdims=True)
    u = lax.broadcasted_iota(jnp.int32,(3*BLK,BLK),0)+(place-2)*BLK
    t = lax.broadcasted_iota(jnp.int32,(3*BLK,BLK),1)+place*BLK
    ok=(u>=0)&(u<=t)&((u>=border)==(t>=border))

    @pl.when(pl.program_id(0) == 0)
    def _():
        bias[...] = jnp.where(ok, 0.0, NEG).astype(f32)

    row_t = lax.broadcasted_iota(jnp.int32,(BLK,HD),0)+place*BLK
    first=jnp.where(row_t<border,1.0,0.0).astype(bf16)
    second=jnp.where(row_t<border,0.0,1.0).astype(bf16)
    first=jnp.concatenate([first]*HEADS_STEP,axis=0); second=jnp.concatenate([second]*HEADS_STEP,axis=0)
    lane_t=lax.broadcasted_iota(jnp.int32,(HD,BLK),1)+place*BLK
    lane_first=jnp.where(lane_t<border,1.0,0.0).astype(bf16)
    lane_first=jnp.concatenate([lane_first]*HEADS_STEP,axis=1)
    lane_second=1-lane_first
    k_p=jnp.concatenate([pr_ref[0,0],pr_ref[1,0]],axis=1)
    v_p=jnp.concatenate([pr_ref[0,1],pr_ref[1,1]],axis=1)
    ks=[k_p, far_ref[0],near_ref[0],kv_ref[0]]
    vs=[v_p, far_ref[1],near_ref[1],kv_ref[1]]
    k_r_t=jnp.concatenate(ks[1:],axis=0).T
    k_p_t=jnp.concatenate([pr_ref[0,0],pr_ref[1,0]],axis=0).T

    st={}
    def cols(pair,j): return pl.ds((HEADS_STEP*pair+j)*HD,HD)
    def load(p):
        q=jnp.concatenate([q_ref[:,cols(p,j)] for j in range(HEADS_STEP)],axis=0)
        do=jnp.concatenate([do_ref[:,cols(p,j)] for j in range(HEADS_STEP)],axis=0)
        return q,do
    def two(x): return jnp.concatenate([x*first,x*second],axis=1)
    def s_chunk(p,c):
        q,_=load(p)
        s=dot_nt(ks[c], two(q) if c==0 else q)
        if c>0:
            bc=bias[(c-1)*BLK:c*BLK]
            s=s+jnp.concatenate([bc]*HEADS_STEP,axis=1)
        ebuf[p%2][c*BLK:(c+1)*BLK]=s
        m=fold(s,jnp.maximum)
        st[p,"top"]=m if c==0 else jnp.maximum(st[p,"top"],m)
        if c==3: st[p,"top"]=jnp.max(st[p,"top"],axis=0,keepdims=True)
    def g_chunk(p,c):
        _,do=load(p)
        gbuf[p%2][c*BLK:(c+1)*BLK]=dot_nt(vs[c], two(do) if c==0 else do)
    def pass2(p,c):
        sl=slice(c*BLK,(c+1)*BLK)
        e=jnp.exp2((ebuf[p%2][sl]-st[p,"top"])*LOG2_SCALE)
        ebuf[p%2][sl]=e
        a1=fold(e,jnp.add); a2=fold(e*gbuf[p%2][sl],jnp.add)
        st[p,"tot"]=a1 if c==0 else st[p,"tot"]+a1
        st[p,"dl"]=a2 if c==0 else st[p,"dl"]+a2
        if c==3:
            st[p,"inv"]=1.0/jnp.sum(st[p,"tot"],axis=0,keepdims=True)
            st[p,"delta"]=jnp.sum(st[p,"dl"],axis=0,keepdims=True)*st[p,"inv"]
    def pass3(p,c):
        sl=slice(c*BLK,(c+1)*BLK)
        w=ebuf[p%2][sl]*st[p,"inv"]
        pbuf[p%2][sl]=w.astype(bf16)
        dsbuf[p%2][sl]=(w*(gbuf[p%2][sl]-st[p,"delta"])).astype(bf16)
    def dq_part(p):
        ds_p=dsbuf[p%2][:BLK]
        ds_two=jnp.concatenate([ds_p*lane_first,ds_p*lane_second],axis=0)
        dq_t=dot_nn(k_r_t,dsbuf[p%2][BLK:])+dot_nn(k_p_t,ds_two)
        dq=(dq_t*FACTOR).T.astype(bf16)
        for j in range(HEADS_STEP):
            dq_ref[:,cols(p,j)]=dq[j*BLK:(j+1)*BLK]
    def dk_part(p,c,kv):
        x=load(p)[kv]
        src=(dsbuf,pbuf)[kv][p%2][c*BLK:(c+1)*BLK]
        r=dot_nn(src, two(x) if c==0 else x)
        acc=(dkacc,dvacc)[kv] if c>0 else (dkpacc,dvpacc)[kv]
        sl=slice((c-1)*BLK,c*BLK) if c>0 else slice(0,BLK)
        if p==0: acc[sl]=r
        else: acc[sl]=acc[sl]+r
    def mk(p):
        l=[]
        for c in range(4):
            l.append(lambda c=c: s_chunk(p,c))
        for c in range(4):
            l.append(lambda c=c: g_chunk(p,c))
        return l
    def md(p):
        l=[lambda: dq_part(p)]
        for kv in range(2):
            for c in range(4): l.append(lambda c=c,kv=kv: dk_part(p,c,kv))
        return l
    def vp(p):
        return [lambda c=c: pass2(p,c) for c in range(4)]+[lambda c=c: pass3(p,c) for c in range(4)]
    def weave(v,m):
        n=max(len(v),1)
        for i in range(n):
            for f in m[len(m)*i//n:len(m)*(i+1)//n]: f()
            if i<len(v): v[i]()
    for f in mk(0): f()
    for p in range(STEPS):
        m=[]
        if p>0: m+=md(p-1)
        if p+1<STEPS: m+=mk(p+1)
        weave(vp(p),m)
    for f in md(STEPS-1): f()
    for j,(r,pp) in enumerate(((dkacc,dkpacc),(dvacc,dvpacc))):
        sc_=FACTOR if j==0 else 1.0
        dfar_ref[j]=(r[:BLK]*sc_).astype(bf16)
        dnear_ref[j]=(r[BLK:2*BLK]*sc_).astype(bf16)
        own_ref[j]=r[2*BLK:]*sc_
        dpr_ref[0,j]=(pp[:,:HD]*sc_).astype(bf16)
        dpr_ref[1,j]=(pp[:,HD:]*sc_).astype(bf16)

def attend(slot, place, seg, q, do, kv, near, far, prompts, carried):
    def head_of(i, sc):
        return 2 * lax.rem(sc[0] + (N_X - slot), N_X) + i

    def at_head(i, sc):
        return (0, head_of(i, sc))

    def pair_at_head(i, sc):
        return (0, 0, head_of(i, sc))

    wide_spec = pl.BlockSpec((BLK, HEAD_COLS), at_head)
    one_spec = pl.BlockSpec((BLK, HD), at_head)
    pair_spec = pl.BlockSpec((2, BLK, HD), pair_at_head)
    prompt_spec = pl.BlockSpec((2, 2, BLK, HD), lambda i, sc: (0, 0, 0, i))
    seg_spec = pl.BlockSpec((1, 512), lambda i, sc: (0, 0))
    out_shape = (
        jax.ShapeDtypeStruct((BLK, KV_HEADS * HEAD_COLS), bf16),
        jax.ShapeDtypeStruct((2, BLK, KV_HEADS * HD), f32),
        jax.ShapeDtypeStruct((2, BLK, KV_HEADS * HD), bf16),
        jax.ShapeDtypeStruct((2, BLK, KV_HEADS * HD), bf16),
        jax.ShapeDtypeStruct((2, 2, BLK, 2 * HD), bf16),
    )
    in_specs = [seg_spec, wide_spec, wide_spec, pair_spec, pair_spec, pair_spec, prompt_spec]
    aliases = {}
    operands = [seg, q, do, kv, near, far, prompts]
    if carried is not None:
        for k, array in enumerate(carried):
            aliases[1 + len(operands)] = k
            operands.append(array)
            in_specs.append(pl.BlockSpec(memory_space=pl.ANY))
    return pl.pallas_call(
        functools.partial(attention_kernel, slot),
        out_shape=out_shape,
        grid_spec=pltpu.PrefetchScalarGridSpec(
            num_scalar_prefetch=1,
            grid=(2,),
            in_specs=in_specs,
            out_specs=(wide_spec, pair_spec, pair_spec, pair_spec, prompt_spec),
            scratch_shapes=[pltpu.VMEM((3 * BLK, BLK), f32)]
            + [pltpu.VMEM((4 * BLK, LANES), f32)] * 4
            + [pltpu.VMEM((4 * BLK, LANES), bf16)] * 4
            + [pltpu.VMEM((3 * BLK, HD), f32)] * 2
            + [pltpu.VMEM((BLK, 2 * HD), f32)] * 2,
        ),
        input_output_aliases=aliases,
        compiler_params=pltpu.CompilerParams(vmem_limit_bytes=12 * 1024 * 1024),
        cost_estimate=pl.CostEstimate(
            flops=5 * 2 * 1024 * 512 * 128 * 2 * 2, bytes_accessed=4 << 20, transcendentals=1 << 20
        ),
    )(place, *operands)


def prepare_kernel(pk_ref, pv_ref, rk_ref, rv_ref, rows_ref, kv_ref):
    kv_ref[0] = rk_ref[...]
    kv_ref[1] = rv_ref[...]
    both = jnp.concatenate([pk_ref[...].astype(f32), pv_ref[...].astype(f32)], axis=0)
    both = both.astype(bf16)
    for i in range(32):
        rows_ref[i] = both


def prepare(pk, pv, rk, rv):
    return pl.pallas_call(
        prepare_kernel,
        out_shape=(
            jax.ShapeDtypeStruct((32, 16, 256), bf16),
            jax.ShapeDtypeStruct((2, BLK, KV_HEADS * HD), bf16),
        ),
        compiler_params=pltpu.CompilerParams(vmem_limit_bytes=56 * 1024 * 1024),
    )(pk, pv, rk, rv)


def pick_kernel(group_ref, core_ref, mine_ref, other_ref, near_ref, far_ref, out_ref):
    first_core = core_ref[0] == 0
    for r in range(2):
        start = group_ref[0, r] * 8
        for j in range(8):
            mine = mine_ref[start + j].astype(f32)
            other = other_ref[start + j].astype(f32)
            even = jnp.where(first_core, mine, other)
            odd = jnp.where(first_core, other, mine)
            for kv in range(2):
                rows = slice(8 * kv, 8 * kv + 8)
                out_ref[r, kv, 16 * j : 16 * j + 16, :] = jnp.concatenate(
                    [even[rows], odd[rows]], axis=0
                ).astype(bf16)


def pick(groups, core, mine, other, near, far):
    whole = pl.BlockSpec((32, 16, 256), lambda i, g, c: (0, 0, 0))
    return pl.pallas_call(
        pick_kernel,
        compiler_params=pltpu.CompilerParams(vmem_limit_bytes=6 * 1024 * 1024),
        out_shape=jax.ShapeDtypeStruct((2, 2, BLK, 256), bf16),
        grid_spec=pltpu.PrefetchScalarGridSpec(
            num_scalar_prefetch=2,
            grid=(1,),
            in_specs=[whole, whole] + [pl.BlockSpec(memory_space=pl.ANY)] * 2,
            out_specs=pl.BlockSpec((2, 2, BLK, 256), lambda i, g, c: (0, 0, 0, 0)),
        ),
    )(groups, core, mine, other, near, far)


def spread_kernel(group_ref, core_ref, a_ref, b_ref, c_ref, d_ref, keep_ref, give_ref):
    first_core = core_ref[0] == 0
    for j in range(8):
        rows = slice(16 * j, 16 * j + 16)
        total = []
        for r in range(2):
            total.append(
                [
                    (a_ref[r, kv, rows].astype(f32) + b_ref[r, kv, rows].astype(f32))
                    + (c_ref[r, kv, rows].astype(f32) + d_ref[r, kv, rows].astype(f32))
                    for kv in range(2)
                ]
            )
        for g in range(4):
            at = [
                jnp.where(group_ref[0, 0] == g, total[0][kv], 0.0)
                + jnp.where(group_ref[0, 1] == g, total[1][kv], 0.0)
                for kv in range(2)
            ]
            even = jnp.concatenate([at[0][:8], at[1][:8]], axis=0)
            odd = jnp.concatenate([at[0][8:], at[1][8:]], axis=0)
            keep_ref[8 * g + j] = jnp.where(first_core, even, odd)
            give_ref[8 * g + j] = jnp.where(first_core, odd, even).astype(bf16)


def spread(groups, core, parts):
    part = pl.BlockSpec((2, 2, BLK, 256), lambda i, g, c: (0, 0, 0, 0))
    whole = pl.BlockSpec((32, 16, 256), lambda i, g, c: (0, 0, 0))
    return pl.pallas_call(
        spread_kernel,
        compiler_params=pltpu.CompilerParams(vmem_limit_bytes=6 * 1024 * 1024),
        out_shape=(
            jax.ShapeDtypeStruct((32, 16, 256), f32),
            jax.ShapeDtypeStruct((32, 16, 256), bf16),
        ),
        grid_spec=pltpu.PrefetchScalarGridSpec(
            num_scalar_prefetch=2, grid=(1,), in_specs=[part] * 4, out_specs=(whole, whole)
        ),
    )(groups, core, *parts)


def shift(a, axis, size, by):
    return lax.ppermute(a, axis, [(i, (i + by) % size) for i in range(size)])


def on_device(q, rk, rv, do, pk, pv, segment_ids, response_group):
    place = lax.axis_index("x").astype(jnp.int32).reshape(1)
    core = lax.axis_index("core").astype(jnp.int32).reshape(1)

    sent, kv = prepare(pk, pv, rk, rv)
    near = lax.ppermute(kv, "x", [(0, 1), (1, 2), (2, 3)])
    far = lax.ppermute(kv, "x", [(0, 2), (1, 3)])

    rows = lax.all_to_all(sent, ("z", "y"), 0, 0)
    rows, near = lax.optimization_barrier((rows, near))
    other = lax.ppermute(rows, "core", [(0, 1), (1, 0)])
    own_prompts = pick(response_group, core, rows, other, near, far)
    slots = [own_prompts] + [shift(own_prompts, "x", N_X, d) for d in range(1, N_X)]

    carried = None
    sent_back = {}
    for d in (0, 1, 2, 3):
        prompts = slots[d]
        if d == 3:
            prompts, sent_back[1] = lax.optimization_barrier((prompts, sent_back[1]))
        *carried, grad_prompts = attend(
            d, place, segment_ids, q, do, kv, near, far, prompts, carried
        )
        sent_back[d] = grad_prompts if d == 0 else shift(grad_prompts, "x", N_X, -d)
    out_q, own, grad_near, grad_far = carried
    back_near = lax.ppermute(grad_near, "x", [(1, 0), (2, 1), (3, 2)])
    back_far = lax.ppermute(grad_far, "x", [(2, 0), (3, 1)])

    keep, give = spread(response_group, core, [sent_back[d] for d in range(N_X)])
    got = lax.ppermute(give, "core", [(0, 1), (1, 0)])
    half = (keep + got.astype(f32)).astype(bf16)
    spread_out = lax.all_to_all(half, ("z", "y"), 0, 0)
    out_p = jnp.sum(spread_out.astype(f32), axis=0)

    out_kv = (own + (back_near.astype(f32) + back_far.astype(f32))).astype(bf16)
    return out_q, out_kv[0], out_kv[1], out_p[:8], out_p[8:]


def solution(mesh):
    fine = Mesh(mesh.devices.reshape(8, 4, 2, 4), ("z", "y", "core", "x"))
    dp = ("z", "y", "core")
    tokens = P(dp + ("x",), None)
    heads = P(dp, "x")
    per_dp = P(dp, None)
    return jax.shard_map(
        on_device,
        mesh=fine,
        in_specs=(tokens, tokens, tokens, tokens, heads, heads, per_dp, per_dp),
        out_specs=(tokens, tokens, tokens, heads, heads),
        check_vma=False,
    )
```

```python
import functools
import functools
import math

import jax
import jax.numpy as jnp
from jax import lax
from jax.experimental import pallas as pl
from jax.experimental.pallas import tpu as pltpu
from jax.sharding import Mesh, PartitionSpec as P

HD = 128
BLK = 128
HEAD_COLS = 1024
KV_HEADS = 8
N_X = 4
FACTOR = HD**-0.5
LOG2_SCALE = FACTOR * math.log2(math.e)
NEG = -1e30
HEADS_STEP = 2
LANES = HEADS_STEP * BLK
STEPS = 4
bf16, f32 = jnp.bfloat16, jnp.float32


def dot_nt(a, b):
    return lax.dot_general(a, b, (((1,), (1,)), ((), ())), preferred_element_type=f32)


def dot_nn(a, b):
    return lax.dot_general(a, b, (((1,), (0,)), ((), ())), preferred_element_type=f32)


def fold(x, op):
    parts=[x[8*i:8*i+8] for i in range(x.shape[0]//8)]
    while len(parts)>1:
        parts=[op(parts[i],parts[i+1]) if i+1<len(parts) else parts[i] for i in range(0,len(parts),2)]
    return parts[0]
def attention_kernel(
    slot, sc_ref, seg_ref, q_ref, do_ref, kv_ref, near_ref, far_ref, pr_ref, *refs):
    dq_ref, own_ref, dnear_ref, dfar_ref, dpr_ref = refs[-18:-13]
    bias, e0,e1,g0,g1,p0,p1,d0,d1,dkacc,dvacc,dkpacc,dvpacc = refs[-13:]
    ebuf,gbuf,pbuf,dsbuf=(e0,e1),(g0,g1),(p0,p1),(d0,d1)
    place = sc_ref[0]
    border = jnp.sum((seg_ref[...] == 0).astype(jnp.int32), axis=1, keepdims=True)
    u = lax.broadcasted_iota(jnp.int32,(3*BLK,BLK),0)+(place-2)*BLK
    t = lax.broadcasted_iota(jnp.int32,(3*BLK,BLK),1)+place*BLK
    ok=(u>=0)&(u<=t)&((u>=border)==(t>=border))

    @pl.when(pl.program_id(0) == 0)
    def _():
        bias[...] = jnp.where(ok, 0.0, NEG).astype(f32)

    row_t = lax.broadcasted_iota(jnp.int32,(BLK,HD),0)+place*BLK
    first=jnp.where(row_t<border,1.0,0.0).astype(bf16)
    second=jnp.where(row_t<border,0.0,1.0).astype(bf16)
    first=jnp.concatenate([first]*HEADS_STEP,axis=0); second=jnp.concatenate([second]*HEADS_STEP,axis=0)
    lane_t=lax.broadcasted_iota(jnp.int32,(HD,BLK),1)+place*BLK
    lane_first=jnp.where(lane_t<border,1.0,0.0).astype(bf16)
    lane_first=jnp.concatenate([lane_first]*HEADS_STEP,axis=1)
    lane_second=1-lane_first
    k_p=jnp.concatenate([pr_ref[0,0],pr_ref[1,0]],axis=1)
    v_p=jnp.concatenate([pr_ref[0,1],pr_ref[1,1]],axis=1)
    ks=[k_p, far_ref[0],near_ref[0],kv_ref[0]]
    vs=[v_p, far_ref[1],near_ref[1],kv_ref[1]]
    k_r=jnp.concatenate(ks[1:],axis=0)
    v_r=jnp.concatenate(vs[1:],axis=0)
    k_r_t=k_r.T
    k_p_t=jnp.concatenate([pr_ref[0,0],pr_ref[1,0]],axis=0).T

    st={}
    def cols(pair,j): return pl.ds((HEADS_STEP*pair+j)*HD,HD)
    def load(p):
        q=jnp.concatenate([q_ref[:,cols(p,j)] for j in range(HEADS_STEP)],axis=0)
        do=jnp.concatenate([do_ref[:,cols(p,j)] for j in range(HEADS_STEP)],axis=0)
        return q,do
    def two(x): return jnp.concatenate([x*first,x*second],axis=1)
    def s_chunk(p,c):
        q,_=load(p)
        if c==0:
            s=dot_nt(k_p,two(q))
            ebuf[p%2][:BLK]=s
            st[p,"top"]=fold(s,jnp.maximum)
        else:
            s=dot_nt(k_r,q)+jnp.concatenate([bias[...]]*HEADS_STEP,axis=1)
            ebuf[p%2][BLK:]=s
            for j in range(3): st[p,"top"]=jnp.maximum(st[p,"top"],fold(s[j*BLK:(j+1)*BLK],jnp.maximum))
        if c==1: st[p,"top"]=jnp.max(st[p,"top"],axis=0,keepdims=True)
    def g_chunk(p,c):
        _,do=load(p)
        if c==0: gbuf[p%2][:BLK]=dot_nt(v_p,two(do))
        else: gbuf[p%2][BLK:]=dot_nt(v_r,do)
    def pass2(p,c):
        sl=slice(c*BLK,(c+1)*BLK)
        e=jnp.exp2((ebuf[p%2][sl]-st[p,"top"])*LOG2_SCALE)
        ebuf[p%2][sl]=e
        a1=fold(e,jnp.add); a2=fold(e*gbuf[p%2][sl],jnp.add)
        st[p,"tot"]=a1 if c==0 else st[p,"tot"]+a1
        st[p,"dl"]=a2 if c==0 else st[p,"dl"]+a2
        if c==3:
            st[p,"inv"]=1.0/jnp.sum(st[p,"tot"],axis=0,keepdims=True)
            st[p,"delta"]=jnp.sum(st[p,"dl"],axis=0,keepdims=True)*st[p,"inv"]
    def pass3(p,c):
        sl=slice(c*BLK,(c+1)*BLK)
        w=ebuf[p%2][sl]*st[p,"inv"]
        pbuf[p%2][sl]=w.astype(bf16)
        dsbuf[p%2][sl]=(w*(gbuf[p%2][sl]-st[p,"delta"])).astype(bf16)
    def dq_part(p):
        ds_p=dsbuf[p%2][:BLK]
        ds_two=jnp.concatenate([ds_p*lane_first,ds_p*lane_second],axis=0)
        dq_t=dot_nn(k_r_t,dsbuf[p%2][BLK:])+dot_nn(k_p_t,ds_two)
        dq=(dq_t*FACTOR).T.astype(bf16)
        for j in range(HEADS_STEP):
            dq_ref[:,cols(p,j)]=dq[j*BLK:(j+1)*BLK]
    def dk_part(p,c,kv):
        x=load(p)[kv]
        sr=slice(0,BLK) if c==0 else slice(BLK,4*BLK)
        src=(dsbuf,pbuf)[kv][p%2][sr]
        r=dot_nn(src, two(x) if c==0 else x)
        acc=(dkacc,dvacc)[kv] if c>0 else (dkpacc,dvpacc)[kv]
        sl=slice(0,3*BLK) if c>0 else slice(0,BLK)
        if p==0: acc[sl]=r
        else: acc[sl]=acc[sl]+r
    def mk(p):
        l=[]
        for c in range(2):
            l.append(lambda c=c: s_chunk(p,c))
        for c in range(2):
            l.append(lambda c=c: g_chunk(p,c))
        return l
    def md(p):
        l=[lambda: dq_part(p)]
        for kv in range(2):
            for c in range(2): l.append(lambda c=c,kv=kv: dk_part(p,c,kv))
        return l
    def vp(p):
        return [lambda c=c: pass2(p,c) for c in range(4)]+[lambda c=c: pass3(p,c) for c in range(4)]
    def weave(v,m):
        n=max(len(v),1)
        for i in range(n):
            for f in m[len(m)*i//n:len(m)*(i+1)//n]: f()
            if i<len(v): v[i]()
    for f in mk(0): f()
    for p in range(STEPS):
        m=[]
        if p>0: m+=md(p-1)
        if p+1<STEPS: m+=mk(p+1)
        weave(vp(p),m)
    for f in md(STEPS-1): f()
    for j,(r,pp) in enumerate(((dkacc,dkpacc),(dvacc,dvpacc))):
        sc_=FACTOR if j==0 else 1.0
        dfar_ref[j]=(r[:BLK]*sc_).astype(bf16)
        dnear_ref[j]=(r[BLK:2*BLK]*sc_).astype(bf16)
        own_ref[j]=r[2*BLK:]*sc_
        dpr_ref[0,j]=(pp[:,:HD]*sc_).astype(bf16)
        dpr_ref[1,j]=(pp[:,HD:]*sc_).astype(bf16)

def attend(slot, place, seg, q, do, kv, near, far, prompts, carried):
    def head_of(i, sc):
        return 2 * lax.rem(sc[0] + (N_X - slot), N_X) + i

    def at_head(i, sc):
        return (0, head_of(i, sc))

    def pair_at_head(i, sc):
        return (0, 0, head_of(i, sc))

    wide_spec = pl.BlockSpec((BLK, HEAD_COLS), at_head)
    one_spec = pl.BlockSpec((BLK, HD), at_head)
    pair_spec = pl.BlockSpec((2, BLK, HD), pair_at_head)
    prompt_spec = pl.BlockSpec((2, 2, BLK, HD), lambda i, sc: (0, 0, 0, i))
    seg_spec = pl.BlockSpec((1, 512), lambda i, sc: (0, 0))
    out_shape = (
        jax.ShapeDtypeStruct((BLK, KV_HEADS * HEAD_COLS), bf16),
        jax.ShapeDtypeStruct((2, BLK, KV_HEADS * HD), f32),
        jax.ShapeDtypeStruct((2, BLK, KV_HEADS * HD), bf16),
        jax.ShapeDtypeStruct((2, BLK, KV_HEADS * HD), bf16),
        jax.ShapeDtypeStruct((2, 2, BLK, 2 * HD), bf16),
    )
    in_specs = [seg_spec, wide_spec, wide_spec, pair_spec, pair_spec, pair_spec, prompt_spec]
    aliases = {}
    operands = [seg, q, do, kv, near, far, prompts]
    if carried is not None:
        for k, array in enumerate(carried):
            aliases[1 + len(operands)] = k
            operands.append(array)
            in_specs.append(pl.BlockSpec(memory_space=pl.ANY))
    return pl.pallas_call(
        functools.partial(attention_kernel, slot),
        out_shape=out_shape,
        grid_spec=pltpu.PrefetchScalarGridSpec(
            num_scalar_prefetch=1,
            grid=(2,),
            in_specs=in_specs,
            out_specs=(wide_spec, pair_spec, pair_spec, pair_spec, prompt_spec),
            scratch_shapes=[pltpu.VMEM((3 * BLK, BLK), f32)]
            + [pltpu.VMEM((4 * BLK, LANES), f32)] * 4
            + [pltpu.VMEM((4 * BLK, LANES), bf16)] * 4
            + [pltpu.VMEM((3 * BLK, HD), f32)] * 2
            + [pltpu.VMEM((BLK, 2 * HD), f32)] * 2,
        ),
        input_output_aliases=aliases,
        compiler_params=pltpu.CompilerParams(vmem_limit_bytes=48 * 1024 * 1024),
        cost_estimate=pl.CostEstimate(
            flops=5 * 2 * 1024 * 512 * 128 * 2 * 2, bytes_accessed=4 << 20, transcendentals=1 << 20
        ),
    )(place, *operands)


def prepare_kernel(pk_ref, pv_ref, rk_ref, rv_ref, rows_ref, kv_ref):
    kv_ref[0] = rk_ref[...]
    kv_ref[1] = rv_ref[...]
    both = jnp.concatenate([pk_ref[...].astype(f32), pv_ref[...].astype(f32)], axis=0)
    both = both.astype(bf16)
    for i in range(32):
        rows_ref[i] = both


def prepare(pk, pv, rk, rv):
    return pl.pallas_call(
        prepare_kernel,
        out_shape=(
            jax.ShapeDtypeStruct((32, 16, 256), bf16),
            jax.ShapeDtypeStruct((2, BLK, KV_HEADS * HD), bf16),
        ),
        compiler_params=pltpu.CompilerParams(vmem_limit_bytes=56 * 1024 * 1024),
    )(pk, pv, rk, rv)


def pick_kernel(group_ref, core_ref, mine_ref, other_ref, near_ref, far_ref, out_ref):
    first_core = core_ref[0] == 0
    for r in range(2):
        start = group_ref[0, r] * 8
        for j in range(8):
            mine = mine_ref[start + j].astype(f32)
            other = other_ref[start + j].astype(f32)
            even = jnp.where(first_core, mine, other)
            odd = jnp.where(first_core, other, mine)
            for kv in range(2):
                rows = slice(8 * kv, 8 * kv + 8)
                out_ref[r, kv, 16 * j : 16 * j + 16, :] = jnp.concatenate(
                    [even[rows], odd[rows]], axis=0
                ).astype(bf16)


def pick(groups, core, mine, other, near, far):
    whole = pl.BlockSpec((32, 16, 256), lambda i, g, c: (0, 0, 0))
    return pl.pallas_call(
        pick_kernel,
        compiler_params=pltpu.CompilerParams(vmem_limit_bytes=6 * 1024 * 1024),
        out_shape=jax.ShapeDtypeStruct((2, 2, BLK, 256), bf16),
        grid_spec=pltpu.PrefetchScalarGridSpec(
            num_scalar_prefetch=2,
            grid=(1,),
            in_specs=[whole, whole] + [pl.BlockSpec(memory_space=pl.ANY)] * 2,
            out_specs=pl.BlockSpec((2, 2, BLK, 256), lambda i, g, c: (0, 0, 0, 0)),
        ),
    )(groups, core, mine, other, near, far)


def spread_kernel(group_ref, core_ref, a_ref, b_ref, c_ref, d_ref, keep_ref, give_ref):
    first_core = core_ref[0] == 0
    for j in range(8):
        rows = slice(16 * j, 16 * j + 16)
        total = []
        for r in range(2):
            total.append(
                [
                    (a_ref[r, kv, rows].astype(f32) + b_ref[r, kv, rows].astype(f32))
                    + (c_ref[r, kv, rows].astype(f32) + d_ref[r, kv, rows].astype(f32))
                    for kv in range(2)
                ]
            )
        for g in range(4):
            at = [
                jnp.where(group_ref[0, 0] == g, total[0][kv], 0.0)
                + jnp.where(group_ref[0, 1] == g, total[1][kv], 0.0)
                for kv in range(2)
            ]
            even = jnp.concatenate([at[0][:8], at[1][:8]], axis=0)
            odd = jnp.concatenate([at[0][8:], at[1][8:]], axis=0)
            keep_ref[8 * g + j] = jnp.where(first_core, even, odd)
            give_ref[8 * g + j] = jnp.where(first_core, odd, even).astype(bf16)


def spread(groups, core, parts):
    part = pl.BlockSpec((2, 2, BLK, 256), lambda i, g, c: (0, 0, 0, 0))
    whole = pl.BlockSpec((32, 16, 256), lambda i, g, c: (0, 0, 0))
    return pl.pallas_call(
        spread_kernel,
        compiler_params=pltpu.CompilerParams(vmem_limit_bytes=6 * 1024 * 1024),
        out_shape=(
            jax.ShapeDtypeStruct((32, 16, 256), f32),
            jax.ShapeDtypeStruct((32, 16, 256), bf16),
        ),
        grid_spec=pltpu.PrefetchScalarGridSpec(
            num_scalar_prefetch=2, grid=(1,), in_specs=[part] * 4, out_specs=(whole, whole)
        ),
    )(groups, core, *parts)


def shift(a, axis, size, by):
    return lax.ppermute(a, axis, [(i, (i + by) % size) for i in range(size)])


def on_device(q, rk, rv, do, pk, pv, segment_ids, response_group):
    place = lax.axis_index("x").astype(jnp.int32).reshape(1)
    core = lax.axis_index("core").astype(jnp.int32).reshape(1)

    sent, kv = prepare(pk, pv, rk, rv)
    near = lax.ppermute(kv, "x", [(0, 1), (1, 2), (2, 3)])
    far = lax.ppermute(kv, "x", [(0, 2), (1, 3)])

    rows = lax.all_to_all(sent, ("z", "y"), 0, 0)
    rows, near = lax.optimization_barrier((rows, near))
    other = lax.ppermute(rows, "core", [(0, 1), (1, 0)])
    own_prompts = pick(response_group, core, rows, other, near, far)
    slots = [own_prompts] + [shift(own_prompts, "x", N_X, d) for d in range(1, N_X)]

    carried = None
    sent_back = {}
    for d in (0, 1, 2, 3):
        prompts = slots[d]
        if d == 3:
            prompts, sent_back[1] = lax.optimization_barrier((prompts, sent_back[1]))
        *carried, grad_prompts = attend(
            d, place, segment_ids, q, do, kv, near, far, prompts, carried
        )
        sent_back[d] = grad_prompts if d == 0 else shift(grad_prompts, "x", N_X, -d)
    out_q, own, grad_near, grad_far = carried
    back_near = lax.ppermute(grad_near, "x", [(1, 0), (2, 1), (3, 2)])

    keep, give = spread(response_group, core, [sent_back[d] for d in range(N_X)])
    give, grad_far = lax.optimization_barrier((give, grad_far))
    back_far = lax.ppermute(grad_far, "x", [(2, 0), (3, 1)])
    got = lax.ppermute(give, "core", [(0, 1), (1, 0)])
    half = (keep + got.astype(f32)).astype(bf16)
    spread_out = lax.all_to_all(half, ("z", "y"), 0, 0)
    out_p = jnp.sum(spread_out.astype(f32), axis=0)

    out_kv = (own + (back_near.astype(f32) + back_far.astype(f32))).astype(bf16)
    return out_q, out_kv[0], out_kv[1], out_p[:8], out_p[8:]


def solution(mesh):
    fine = Mesh(mesh.devices.reshape(8, 4, 2, 4), ("z", "y", "core", "x"))
    dp = ("z", "y", "core")
    tokens = P(dp + ("x",), None)
    heads = P(dp, "x")
    per_dp = P(dp, None)
    return jax.shard_map(
        on_device,
        mesh=fine,
        in_specs=(tokens, tokens, tokens, tokens, heads, heads, per_dp, per_dp),
        out_specs=(tokens, tokens, tokens, heads, heads),
        check_vma=False,
    )
```

```python
import functools
import functools
import math

import jax
import jax.numpy as jnp
from jax import lax
from jax.experimental import pallas as pl
from jax.experimental.pallas import tpu as pltpu
from jax.sharding import Mesh, PartitionSpec as P

HD = 128
BLK = 128
HEAD_COLS = 1024
KV_HEADS = 8
N_X = 4
FACTOR = HD**-0.5
LOG2_SCALE = FACTOR * math.log2(math.e)
NEG = -1e30
HEADS_STEP = 2
LANES = HEADS_STEP * BLK
STEPS = 4
bf16, f32 = jnp.bfloat16, jnp.float32


def dot_nt(a, b):
    return lax.dot_general(a, b, (((1,), (1,)), ((), ())), preferred_element_type=f32)


def dot_nn(a, b):
    return lax.dot_general(a, b, (((1,), (0,)), ((), ())), preferred_element_type=f32)


def fold(x, op):
    parts=[x[8*i:8*i+8] for i in range(x.shape[0]//8)]
    while len(parts)>1:
        parts=[op(parts[i],parts[i+1]) if i+1<len(parts) else parts[i] for i in range(0,len(parts),2)]
    return parts[0]
def attention_kernel(
    slot, sc_ref, seg_ref, q_ref, do_ref, kv_ref, near_ref, far_ref, pr_ref, *refs):
    dq_ref, own_ref, dnear_ref, dfar_ref, dpr_ref = refs[-18:-13]
    bias, e0,e1,g0,g1,p0,p1,d0,d1,dkacc,dvacc,dkpacc,dvpacc = refs[-13:]
    ebuf,gbuf,pbuf,dsbuf=(e0,e1),(g0,g1),(p0,p1),(d0,d1)
    place = sc_ref[0]
    border = jnp.sum((seg_ref[...] == 0).astype(jnp.int32), axis=1, keepdims=True)
    u = lax.broadcasted_iota(jnp.int32,(3*BLK,BLK),0)+(place-2)*BLK
    t = lax.broadcasted_iota(jnp.int32,(3*BLK,BLK),1)+place*BLK
    ok=(u>=0)&(u<=t)&((u>=border)==(t>=border))

    @pl.when(pl.program_id(0) == 0)
    def _():
        bias[...] = jnp.where(ok, 0.0, NEG).astype(f32)

    row_t = lax.broadcasted_iota(jnp.int32,(BLK,HD),0)+place*BLK
    first=jnp.where(row_t<border,1.0,0.0).astype(bf16)
    second=jnp.where(row_t<border,0.0,1.0).astype(bf16)
    first=jnp.concatenate([first]*HEADS_STEP,axis=0); second=jnp.concatenate([second]*HEADS_STEP,axis=0)
    lane_t=lax.broadcasted_iota(jnp.int32,(HD,BLK),1)+place*BLK
    lane_first=jnp.where(lane_t<border,1.0,0.0).astype(bf16)
    lane_first=jnp.concatenate([lane_first]*HEADS_STEP,axis=1)
    lane_second=1-lane_first
    k_p=jnp.concatenate([pr_ref[0,0],pr_ref[1,0]],axis=1)
    v_p=jnp.concatenate([pr_ref[0,1],pr_ref[1,1]],axis=1)
    ks=[k_p, far_ref[0],near_ref[0],kv_ref[0]]
    vs=[v_p, far_ref[1],near_ref[1],kv_ref[1]]
    k_r=jnp.concatenate(ks[1:],axis=0)
    v_r=jnp.concatenate(vs[1:],axis=0)
    k_r_t=k_r.T
    k_p_t=jnp.concatenate([pr_ref[0,0],pr_ref[1,0]],axis=0).T

    st={}
    def cols(pair,j): return pl.ds((HEADS_STEP*pair+j)*HD,HD)
    def load(p):
        q=jnp.concatenate([q_ref[:,cols(p,j)] for j in range(HEADS_STEP)],axis=0)
        do=jnp.concatenate([do_ref[:,cols(p,j)] for j in range(HEADS_STEP)],axis=0)
        return q,do
    def two(x): return jnp.concatenate([x*first,x*second],axis=1)
    def s_chunk(p,c):
        q,_=load(p)
        if c==0:
            s=dot_nt(k_p,two(q))
            ebuf[p%2][:BLK]=s
            st[p,"top"]=fold(s,jnp.maximum)
        else:
            s=dot_nt(k_r,q)+jnp.concatenate([bias[...]]*HEADS_STEP,axis=1)
            ebuf[p%2][BLK:]=s
            for j in range(3): st[p,"top"]=jnp.maximum(st[p,"top"],fold(s[j*BLK:(j+1)*BLK],jnp.maximum))
        if c==1: st[p,"top"]=jnp.max(st[p,"top"],axis=0,keepdims=True)
    def g_chunk(p,c):
        _,do=load(p)
        if c==0: gbuf[p%2][:BLK]=dot_nt(v_p,two(do))
        else: gbuf[p%2][BLK:]=dot_nt(v_r,do)
    def pass2(p,c):
        sl=slice(c*BLK,(c+1)*BLK)
        e=jnp.exp2((ebuf[p%2][sl]-st[p,"top"])*LOG2_SCALE)
        ebuf[p%2][sl]=e
        a1=fold(e,jnp.add); a2=fold(e*gbuf[p%2][sl],jnp.add)
        st[p,"tot"]=a1 if c==0 else st[p,"tot"]+a1
        st[p,"dl"]=a2 if c==0 else st[p,"dl"]+a2
        if c==3:
            st[p,"inv"]=1.0/jnp.sum(st[p,"tot"],axis=0,keepdims=True)
            st[p,"delta"]=jnp.sum(st[p,"dl"],axis=0,keepdims=True)*st[p,"inv"]
    def pass3(p,c):
        sl=slice(c*BLK,(c+1)*BLK)
        w=ebuf[p%2][sl]*st[p,"inv"]
        pbuf[p%2][sl]=w.astype(bf16)
        dsbuf[p%2][sl]=(w*(gbuf[p%2][sl]-st[p,"delta"])).astype(bf16)
    def dq_part(p):
        ds_p=dsbuf[p%2][:BLK]
        ds_two=jnp.concatenate([ds_p*lane_first,ds_p*lane_second],axis=0)
        dq_t=dot_nn(k_r_t,dsbuf[p%2][BLK:])+dot_nn(k_p_t,ds_two)
        dq=(dq_t*FACTOR).T.astype(bf16)
        for j in range(HEADS_STEP):
            dq_ref[:,cols(p,j)]=dq[j*BLK:(j+1)*BLK]
    def dk_part(p,c,kv):
        x=load(p)[kv]
        sr=slice(0,BLK) if c==0 else slice(BLK,4*BLK)
        src=(dsbuf,pbuf)[kv][p%2][sr]
        r=dot_nn(src, two(x) if c==0 else x)
        acc=(dkacc,dvacc)[kv] if c>0 else (dkpacc,dvpacc)[kv]
        sl=slice(0,3*BLK) if c>0 else slice(0,BLK)
        if p==0: acc[sl]=r
        else: acc[sl]=acc[sl]+r
    def mk(p):
        l=[]
        for c in range(2):
            l.append(lambda c=c: s_chunk(p,c))
        for c in range(2):
            l.append(lambda c=c: g_chunk(p,c))
        return l
    def md(p):
        l=[lambda: dq_part(p)]
        for kv in range(2):
            for c in range(2): l.append(lambda c=c,kv=kv: dk_part(p,c,kv))
        return l
    def vp(p):
        return [lambda c=c: pass2(p,c) for c in range(4)]+[lambda c=c: pass3(p,c) for c in range(4)]
    def weave(v,m):
        n=max(len(v),1)
        for i in range(n):
            for f in m[len(m)*i//n:len(m)*(i+1)//n]: f()
            if i<len(v): v[i]()
    for f in mk(0): f()
    for p in range(STEPS):
        m=[]
        if p>0: m+=md(p-1)
        if p+1<STEPS: m+=mk(p+1)
        weave(vp(p),m)
    for f in md(STEPS-1): f()
    for j,(r,pp) in enumerate(((dkacc,dkpacc),(dvacc,dvpacc))):
        sc_=FACTOR if j==0 else 1.0
        dfar_ref[j]=(r[:BLK]*sc_).astype(bf16)
        dnear_ref[j]=(r[BLK:2*BLK]*sc_).astype(bf16)
        own_ref[j]=r[2*BLK:]*sc_
        dpr_ref[0,j]=(pp[:,:HD]*sc_).astype(bf16)
        dpr_ref[1,j]=(pp[:,HD:]*sc_).astype(bf16)

def attend(slot, place, seg, q, do, kv, near, far, prompts, carried, start=0, count=2):
    def head_of(i, sc):
        return 2 * lax.rem(sc[0] + (N_X - slot), N_X) + (i + start)

    def at_head(i, sc):
        return (0, head_of(i, sc))

    def pair_at_head(i, sc):
        return (0, 0, head_of(i, sc))

    wide_spec = pl.BlockSpec((BLK, HEAD_COLS), at_head)
    one_spec = pl.BlockSpec((BLK, HD), at_head)
    pair_spec = pl.BlockSpec((2, BLK, HD), pair_at_head)
    prompt_spec = pl.BlockSpec((2, 2, BLK, HD), lambda i, sc: (0, 0, 0, i + start))
    seg_spec = pl.BlockSpec((1, 512), lambda i, sc: (0, 0))
    out_shape = (
        jax.ShapeDtypeStruct((BLK, KV_HEADS * HEAD_COLS), bf16),
        jax.ShapeDtypeStruct((2, BLK, KV_HEADS * HD), f32),
        jax.ShapeDtypeStruct((2, BLK, KV_HEADS * HD), bf16),
        jax.ShapeDtypeStruct((2, BLK, KV_HEADS * HD), bf16),
        jax.ShapeDtypeStruct((2, 2, BLK, 2 * HD), bf16),
    )
    in_specs = [seg_spec, wide_spec, wide_spec, pair_spec, pair_spec, pair_spec, prompt_spec]
    aliases = {}
    operands = [seg, q, do, kv, near, far, prompts]
    if carried is not None:
        for k, array in enumerate(carried):
            aliases[1 + len(operands)] = k
            operands.append(array)
            in_specs.append(pl.BlockSpec(memory_space=pl.ANY))
    return pl.pallas_call(
        functools.partial(attention_kernel, slot),
        out_shape=out_shape,
        grid_spec=pltpu.PrefetchScalarGridSpec(
            num_scalar_prefetch=1,
            grid=(count,),
            in_specs=in_specs,
            out_specs=(wide_spec, pair_spec, pair_spec, pair_spec, prompt_spec),
            scratch_shapes=[pltpu.VMEM((3 * BLK, BLK), f32)]
            + [pltpu.VMEM((4 * BLK, LANES), f32)] * 4
            + [pltpu.VMEM((4 * BLK, LANES), bf16)] * 4
            + [pltpu.VMEM((3 * BLK, HD), f32)] * 2
            + [pltpu.VMEM((BLK, 2 * HD), f32)] * 2,
        ),
        input_output_aliases=aliases,
        compiler_params=pltpu.CompilerParams(vmem_limit_bytes=48 * 1024 * 1024),
        cost_estimate=pl.CostEstimate(
            flops=5 * 2 * 1024 * 512 * 128 * 2 * 2, bytes_accessed=4 << 20, transcendentals=1 << 20
        ),
    )(place, *operands)


def prepare_kernel(pk_ref, pv_ref, rk_ref, rv_ref, rows_ref, kv_ref):
    kv_ref[0] = rk_ref[...]
    kv_ref[1] = rv_ref[...]
    both = jnp.concatenate([pk_ref[...].astype(f32), pv_ref[...].astype(f32)], axis=0)
    both = both.astype(bf16)
    for i in range(32):
        rows_ref[i] = both


def prepare(pk, pv, rk, rv):
    return pl.pallas_call(
        prepare_kernel,
        out_shape=(
            jax.ShapeDtypeStruct((32, 16, 256), bf16),
            jax.ShapeDtypeStruct((2, BLK, KV_HEADS * HD), bf16),
        ),
        compiler_params=pltpu.CompilerParams(vmem_limit_bytes=56 * 1024 * 1024),
    )(pk, pv, rk, rv)


def pick_kernel(group_ref, core_ref, mine_ref, other_ref, near_ref, far_ref, out_ref):
    first_core = core_ref[0] == 0
    for r in range(2):
        start = group_ref[0, r] * 8
        for j in range(8):
            mine = mine_ref[start + j].astype(f32)
            other = other_ref[start + j].astype(f32)
            even = jnp.where(first_core, mine, other)
            odd = jnp.where(first_core, other, mine)
            for kv in range(2):
                rows = slice(8 * kv, 8 * kv + 8)
                out_ref[r, kv, 16 * j : 16 * j + 16, :] = jnp.concatenate(
                    [even[rows], odd[rows]], axis=0
                ).astype(bf16)


def pick(groups, core, mine, other, near, far):
    whole = pl.BlockSpec((32, 16, 256), lambda i, g, c: (0, 0, 0))
    return pl.pallas_call(
        pick_kernel,
        compiler_params=pltpu.CompilerParams(vmem_limit_bytes=6 * 1024 * 1024),
        out_shape=jax.ShapeDtypeStruct((2, 2, BLK, 256), bf16),
        grid_spec=pltpu.PrefetchScalarGridSpec(
            num_scalar_prefetch=2,
            grid=(1,),
            in_specs=[whole, whole] + [pl.BlockSpec(memory_space=pl.ANY)] * 2,
            out_specs=pl.BlockSpec((2, 2, BLK, 256), lambda i, g, c: (0, 0, 0, 0)),
        ),
    )(groups, core, mine, other, near, far)


def spread_kernel(group_ref, core_ref, a_ref, b_ref, c_ref, d_ref, keep_ref, give_ref):
    first_core = core_ref[0] == 0
    for j in range(8):
        rows = slice(16 * j, 16 * j + 16)
        total = []
        for r in range(2):
            total.append(
                [
                    (a_ref[r, kv, rows].astype(f32) + b_ref[r, kv, rows].astype(f32))
                    + (c_ref[r, kv, rows].astype(f32) + d_ref[r, kv, rows].astype(f32))
                    for kv in range(2)
                ]
            )
        for g in range(4):
            at = [
                jnp.where(group_ref[0, 0] == g, total[0][kv], 0.0)
                + jnp.where(group_ref[0, 1] == g, total[1][kv], 0.0)
                for kv in range(2)
            ]
            even = jnp.concatenate([at[0][:8], at[1][:8]], axis=0)
            odd = jnp.concatenate([at[0][8:], at[1][8:]], axis=0)
            keep_ref[8 * g + j] = jnp.where(first_core, even, odd)
            give_ref[8 * g + j] = jnp.where(first_core, odd, even).astype(bf16)


def spread(groups, core, parts):
    part = pl.BlockSpec((2, 2, BLK, 256), lambda i, g, c: (0, 0, 0, 0))
    whole = pl.BlockSpec((32, 16, 256), lambda i, g, c: (0, 0, 0))
    return pl.pallas_call(
        spread_kernel,
        compiler_params=pltpu.CompilerParams(vmem_limit_bytes=6 * 1024 * 1024),
        out_shape=(
            jax.ShapeDtypeStruct((32, 16, 256), f32),
            jax.ShapeDtypeStruct((32, 16, 256), bf16),
        ),
        grid_spec=pltpu.PrefetchScalarGridSpec(
            num_scalar_prefetch=2, grid=(1,), in_specs=[part] * 4, out_specs=(whole, whole)
        ),
    )(groups, core, *parts)


def shift(a, axis, size, by):
    return lax.ppermute(a, axis, [(i, (i + by) % size) for i in range(size)])


def on_device(q, rk, rv, do, pk, pv, segment_ids, response_group):
    place = lax.axis_index("x").astype(jnp.int32).reshape(1)
    core = lax.axis_index("core").astype(jnp.int32).reshape(1)

    sent, kv = prepare(pk, pv, rk, rv)
    near = lax.ppermute(kv, "x", [(0, 1), (1, 2), (2, 3)])
    far = lax.ppermute(kv, "x", [(0, 2), (1, 3)])

    rows = lax.all_to_all(sent, ("z", "y"), 0, 0)
    rows, near = lax.optimization_barrier((rows, near))
    other = lax.ppermute(rows, "core", [(0, 1), (1, 0)])
    own_prompts = pick(response_group, core, rows, other, near, far)
    slots = [own_prompts] + [shift(own_prompts, "x", N_X, d) for d in range(1, N_X)]

    carried = None
    sent_back = {}
    inputs = (place, segment_ids, q, do, kv, near, far)
    *carried, own_grad = attend(0, *inputs, slots[0], None, 0, 1)
    for d in (1, 2, 3):
        prompts = slots[d]
        if d == 3:
            prompts, sent_back[1] = lax.optimization_barrier((prompts, sent_back[1]))
        *carried, grad_prompts = attend(d, *inputs, prompts, carried)
        sent_back[d] = shift(grad_prompts, "x", N_X, -d)
    *carried, sent_back[0] = attend(0, *inputs, slots[0], [*carried, own_grad], 1, 1)
    out_q, own, grad_near, grad_far = carried
    back_near = lax.ppermute(grad_near, "x", [(1, 0), (2, 1), (3, 2)])

    keep, give = spread(response_group, core, [sent_back[d] for d in range(N_X)])
    give, grad_far = lax.optimization_barrier((give, grad_far))
    back_far = lax.ppermute(grad_far, "x", [(2, 0), (3, 1)])
    got = lax.ppermute(give, "core", [(0, 1), (1, 0)])
    half = (keep + got.astype(f32)).astype(bf16)
    spread_out = lax.all_to_all(half, ("z", "y"), 0, 0)
    out_p = jnp.sum(spread_out.astype(f32), axis=0)

    out_kv = (own + (back_near.astype(f32) + back_far.astype(f32))).astype(bf16)
    return out_q, out_kv[0], out_kv[1], out_p[:8], out_p[8:]


def solution(mesh):
    fine = Mesh(mesh.devices.reshape(8, 4, 2, 4), ("z", "y", "core", "x"))
    dp = ("z", "y", "core")
    tokens = P(dp + ("x",), None)
    heads = P(dp, "x")
    per_dp = P(dp, None)
    return jax.shard_map(
        on_device,
        mesh=fine,
        in_specs=(tokens, tokens, tokens, tokens, heads, heads, per_dp, per_dp),
        out_specs=(tokens, tokens, tokens, heads, heads),
        check_vma=False,
    )
```
